1024 devices in a mesh: row: 64 (over x, z_hi, y), col: 16 (over z_lo, core).
Axes of the slice: x: 4, y: 8, z: 16 (z_hi: 2, z_lo: 8; z = z_hi * 8 + z_lo), core: 2. Of those that a mesh axis runs over, the one named last changes fastest.
Arguments:
- blocks: float32 [2048, 8, 128, 128], P(('row', 'col')), as said below
- block_cols: int32 [2048, 8], P(('row', 'col')), may hold values from 0 to 2047, as said below
- pair_blocks: int32 [2048, 8, 8], P(('row', 'col')), may hold values from -1 to 2047, as said below
Outputs:
- purified: float32 [2048, 8, 128, 128], P(('row', 'col'))
The draws below stay inside these ranges and needn't reach their ends.
Inputs may be any that keep to these rules, and one draw needn't show every extreme that they name: `block_cols`: row i's 8 columns are (i + d) modulo 2048 for 8 distinct d between -4 and 4, d = 0 always among them, listed in rising d; the pattern is symmetric: j is a column of row i exactly when i is a column of row j. `pair_blocks`: for block (i, s) with column j: every k such that both (i, k) and (k, j) are in the pattern, each once, in rising (k - i) modulo 2048 taken between -4 and 4, then -1s; every diagonal block lists 8 of them. `blocks`: the block at (j, i) is the transpose of the block at (i, j).
All inputs are finite; a program needn't handle non-finite values.
Results may differ from the reference program's by a relative error of at most 0.00005.
Values sent between devices are 32-bit elements; how exact they have to be, the bound alone decides.
No kernel may reach another device: no remote copies, remote signals or barrier semaphores. Data moves between devices by JAX's collectives and lax.ppermute only.
A program may use at most 64 MiB of HBM per device.

```python
import jax
import jax.numpy as jnp
from jax import lax

B = 128
NNZ = 8
REACH = 4
MAXP = 8
NB = 2048


def missing_offsets(key):
    offset_table = jnp.array([[1, -1, 1, -1], [2, 2, -2, -2], [3, 1, -1, -3]], jnp.int32)
    group_picks = jax.random.randint(key, (NB // 4,), 0, 3)
    return offset_table[group_picks].reshape(NB).astype(jnp.int32)


def slot_offsets(missing):
    slot_range = jnp.arange(NNZ, dtype=jnp.int32)[None, :] - REACH
    return jnp.where(slot_range < missing[:, None], slot_range, slot_range + 1).astype(jnp.int32)


def draw_block_cols(key, part):
    missing = missing_offsets(key)
    row_ids = jnp.arange(NB, dtype=jnp.int32)
    return jnp.mod(row_ids[:, None] + slot_offsets(missing), NB).astype(jnp.int32)


def draw_pair_blocks(key, part):
    missing = missing_offsets(key)
    row_ids = jnp.arange(NB, dtype=jnp.int32)
    offsets = slot_offsets(missing)
    step_values = jnp.arange(-REACH, REACH + 1, dtype=jnp.int32)
    step_index = jnp.arange(2 * REACH + 1, dtype=jnp.int32)
    partner_rows = jnp.mod(row_ids[:, None] + step_values[None, :], NB)
    partner_missing = missing[partner_rows]
    gap = offsets[:, :, None] - step_values[None, None, :]
    valid = (step_values[None, None, :] != missing[:, None, None]) & (jnp.abs(gap) <= REACH) & (gap != partner_missing[:, None, :])
    order_scores = jnp.where(valid, step_index[None, None, :], 2 * REACH + 1 + step_index[None, None, :])
    order = jnp.argsort(order_scores, axis=-1, stable=True)
    listed = jnp.where(valid, partner_rows[:, None, :], -1)
    arranged = jnp.take_along_axis(listed, order, axis=-1)
    return arranged[:, :, :MAXP].astype(jnp.int32)


def draw_blocks(key, part):
    missing = missing_offsets(key)
    key = jax.random.fold_in(key, 7)
    raw_values = jax.random.normal(key, (NB, NNZ, B, B), jnp.float32)
    offsets = slot_offsets(missing)
    row_ids = jnp.arange(NB, dtype=jnp.int32)
    mirror_rows = jnp.mod(row_ids[:, None] + offsets, NB)
    back_offsets = -offsets
    mirror_slots = back_offsets + REACH - (missing[mirror_rows] < back_offsets).astype(jnp.int32)
    partner = jnp.swapaxes(raw_values[mirror_rows, mirror_slots], -1, -2)
    scale_factor = 0.4 / (8.0 * B) ** 0.25
    return (scale_factor * (raw_values + partner)).astype(jnp.float32)


def setup_inputs(seed: int = 0) -> dict:
    streams_of = jax.random.split(jax.random.key(seed), 4)
    return {
        "blocks": draw_blocks(jax.random.fold_in(streams_of[3], 71), 0),
        "block_cols": draw_block_cols(jax.random.fold_in(streams_of[3], 71), 0),
        "pair_blocks": draw_pair_blocks(jax.random.fold_in(streams_of[3], 71), 0),
    }


def pick_slots(candidates, wanted):
    slot_range = jnp.arange(candidates.shape[-1], dtype=jnp.int32)
    return jnp.sum(jnp.where(candidates == wanted[..., None], slot_range, 0), axis=-1).astype(jnp.int32)


def reference(blocks, block_cols, pair_blocks):
    column_ids = block_cols.astype(jnp.int32)
    present = pair_blocks >= 0
    summed = jnp.where(present, pair_blocks, 0).astype(jnp.int32)
    left_slot = pick_slots(column_ids[:, None, None, :], summed)
    right_slot = pick_slots(column_ids[summed], column_ids[:, :, None])
    row_ids = jnp.arange(NB, dtype=jnp.int32)[:, None, None]
    left_index = (row_ids * NNZ + left_slot).astype(jnp.int32)
    right_index = (summed * NNZ + right_slot).astype(jnp.int32)
    weights = present.astype(blocks.dtype)
    flat_blocks = blocks.reshape(NB * NNZ, B, B)

    def product(left_flat):
        def one_row(row_items):
            left_ids, right_ids, row_weights = row_items
            left_part = left_flat[left_ids] * row_weights[..., None, None]
            right_part = flat_blocks[right_ids]
            return jnp.einsum("stab,stbc->sac", left_part, right_part, precision=lax.Precision.HIGHEST)

        return lax.map(one_row, (left_index, right_index, weights))

    square = product(flat_blocks)
    cubed = product(square.reshape(NB * NNZ, B, B))
    return 3.0 * square - 2.0 * cubed
```

```python
import jax
import jax.numpy as jnp
from jax import lax
from jax.experimental import pallas as pl
from jax.experimental.pallas import tpu as pltpu
from jax.sharding import PartitionSpec as P

B = 128
NNZ = 8
REACH = 4
ROWS = 2
SPAN = ROWS + 2 * REACH
PAIR = 2 * B
AXES = ("row", "col")
PACKED = 2 * B + 8
DOWN = PACKED + 4 * B
UP = DOWN + 3 * B
NEAR1, NEAR2 = DOWN + 16, DOWN + 8
LATE = 4
BF, F32 = jnp.bfloat16, jnp.float32
SMEM = pl.BlockSpec(memory_space=pltpu.SMEM)
VMEM = pl.BlockSpec(memory_space=pltpu.VMEM)
ANY = pl.BlockSpec(memory_space=pl.ANY)


def device_index():
    return lax.axis_index("row") * lax.axis_size("col") + lax.axis_index("col")


def missing_of(cols_ref, first_row, total_rows):
    found = []
    for i in range(ROWS):
        count = jnp.int32(0)
        for s in range(NNZ):
            natural = lax.rem(first_row + i + s - REACH + total_rows, total_rows)
            count = count + jnp.where(cols_ref[i, s] == natural, 1, 0)
        found.append(count)
    return found


def held(missing, offset):
    return offset != missing


def slot_of(missing, offset):
    return jnp.minimum(offset - jnp.where(missing < offset, 1, 0), NNZ - 1)


def own_block(blocks_ref, missing, i, offset):
    value = blocks_ref[i, slot_of(missing[i], offset)]
    return jnp.where(held(missing[i], offset), value, 0.0)


def grid_ids():
    return lax.broadcasted_iota(jnp.int32, (B, B), 0), lax.broadcasted_iota(jnp.int32, (B, B), 1)


def write_triangle(blocks_ref, missing, out_ref):
    first = own_block(blocks_ref, missing, 0, REACH)
    second = own_block(blocks_ref, missing, 1, REACH)
    rows, cols = grid_ids()
    out_ref[0:B] = jnp.where(rows <= cols, first, second)
    out_ref[B : 2 * B] = own_block(blocks_ref, missing, 0, REACH + 1)
    diagonal = jnp.sum(jnp.where(rows == cols, second, 0.0), axis=0, keepdims=True)
    out_ref[2 * B : PACKED] = jnp.broadcast_to(diagonal, (PACKED - 2 * B, B))


def read_triangle(ref):
    packed, between = ref[0:B], ref[B : 2 * B]
    turned = packed.T
    rows, cols = grid_ids()
    first = jnp.where(rows <= cols, packed, turned)
    second = jnp.where(rows > cols, packed, jnp.where(rows < cols, turned, ref[2 * B : 2 * B + 1]))
    return first, between, second


def pack_up(
    total_rows, blocks_hbm, cols_hbm, up_ref, tri_ref, blocks_ref, cols_ref, blocks_sem, cols_sem
):
    fetch_cols = pltpu.make_async_copy(cols_hbm, cols_ref, cols_sem)
    fetch_blocks = pltpu.make_async_copy(blocks_hbm, blocks_ref, blocks_sem)
    fetch_cols.start()
    fetch_blocks.start()
    fetch_cols.wait()
    missing = missing_of(cols_ref, device_index() * ROWS, total_rows)
    fetch_blocks.wait()
    write_triangle(blocks_ref, missing, tri_ref)
    up_ref[0:PACKED] = tri_ref[...]
    below = ((0, -2), (0, -1), (1, -2), (1, -1))
    across = ((1, 4), (1, 5), (0, 4))
    for n, (i, j) in enumerate(below + across):
        at = PACKED + n * B
        up_ref[at : at + B] = own_block(blocks_ref, missing, i, j - i + REACH)


def pack_down(
    total_rows, blocks_ref, cols_ref, tri_in_ref, near1_ref, near2_ref, last1_ref, last2_ref
):
    missing = missing_of(cols_ref, device_index() * ROWS, total_rows)
    for ref in (near1_ref, near2_ref, last1_ref, last2_ref):
        ref[0:PACKED] = tri_in_ref[...]
    for n, (i, j) in enumerate(((0, 2), (0, 3), (1, 2), (1, 3))):
        at = PACKED + n * B
        value = own_block(blocks_ref, missing, i, j - i + REACH)
        near1_ref[at : at + B] = value
        last1_ref[at : at + B] = value


def pass_on(up1_ref, up2_ref, up1_out_ref, up2_out_ref):
    pass


def tile(n):
    return slice(n * B, (n + 1) * B)


def purify(
    total_rows,
    blocks_ref,
    cols_ref,
    up1_ref,
    up2_ref,
    down1_ref,
    down2_ref,
    out_hbm,
    high,
    low,
    square,
    square_high,
    square_low,
    staged,
    out_sem,
):
    missing = missing_of(cols_ref, device_index() * ROWS, total_rows)

    def put(k, j, value):
        top = value.astype(BF)
        high[tile(k), tile(j)] = top
        low[tile(k), tile(j)] = (value - top.astype(F32)).astype(BF)

    def put_both(k, j, value):
        put(k, j, value)
        put(j, k, value.T)

    for i in range(ROWS):
        for offset in range(2 * REACH + 1):
            value = own_block(blocks_ref, missing, i, offset)
            j = i + offset
            if REACH <= j < REACH + ROWS:
                put(REACH + i, j, value)
            else:
                put_both(REACH + i, j, value)
    for ref, at in ((up2_ref, 0), (up1_ref, 2), (down1_ref, 6), (down2_ref, 8)):
        first, between, second = read_triangle(ref)
        put(at, at, first)
        put_both(at, at + 1, between)
        put(at + 1, at + 1, second)
    for n, (k, j) in enumerate(((2, 0), (2, 1), (3, 0), (3, 1))):
        put_both(k, j, up1_ref[PACKED + n * B : PACKED + (n + 1) * B])
    for n, (k, j) in enumerate(((6, 8), (6, 9), (7, 8), (7, 9))):
        put_both(k, j, down1_ref[PACKED + n * B : PACKED + (n + 1) * B])
    for n, (k, j) in enumerate(((3, 6), (3, 7), (2, 6))):
        put_both(k, j, up1_ref[DOWN + n * B : DOWN + (n + 1) * B])
    nothing = jnp.zeros((B, B), BF)
    for k, j in ((0, 5), (2, 7), (4, 9)):
        for part in (high, low):
            part[tile(k), tile(j)] = nothing
            part[tile(j), tile(k)] = nothing

    def product(left_high, left_low, b):
        inner = slice(max(0, b - 2) * PAIR, min(SPAN // 2, b + 3) * PAIR)
        outer = slice(b * PAIR, (b + 1) * PAIR)

        def dot(left, right):
            return jnp.dot(left, right[inner, outer], preferred_element_type=F32)

        return dot(left_high(inner), high) + dot(left_low(inner), high) + dot(left_high(inner), low)

    own = slice(REACH * B, (REACH + ROWS) * B)
    for b in range(SPAN // 2):
        total = product(lambda at: high[own, at], lambda at: low[own, at], b)
        for i in range(ROWS):
            for j in (2 * b, 2 * b + 1):
                value = total[tile(i), tile(j - 2 * b)]
                offset = j - i
                if 0 <= offset <= 2 * REACH:
                    value = jnp.where(held(missing[i], offset), value, 0.0)
                else:
                    value = jnp.zeros_like(value)
                square[tile(i), tile(j)] = value
                top = value.astype(BF)
                square_high[tile(i), tile(j)] = top
                square_low[tile(i), tile(j)] = (value - top.astype(F32)).astype(BF)
    for b in range(SPAN // 2):
        total = product(lambda at: square_high[:, at], lambda at: square_low[:, at], b)
        outer = slice(b * PAIR, (b + 1) * PAIR)
        square[:, outer] = 3.0 * square[:, outer] - 2.0 * total
        for i in range(ROWS):
            for s in range(NNZ):
                if (i + s + 1) // 2 == b:
                    at = pl.multiple_of((i + s + jnp.where(missing[i] <= s, 1, 0)) * B, B)
                    staged[i, s] = square[tile(i), pl.ds(at, B)]
                    pltpu.make_async_copy(staged.at[i, s], out_hbm.at[i, s], out_sem).start()
    pltpu.make_async_copy(staged, out_hbm, out_sem).wait()


def late():
    return lax.axis_index("col") >= lax.axis_size("col") - LATE


def purify_most(total_rows, *refs):
    @pl.when(jnp.logical_not(late()))
    def _():
        purify(total_rows, *refs)


def purify_last(
    total_rows,
    blocks_ref,
    cols_ref,
    up1_ref,
    up2_ref,
    down1_ref,
    down2_ref,
    last1_ref,
    last2_ref,
    given_ref,
    *refs,
):
    @pl.when(late())
    def _():
        @pl.when(lax.axis_index("col") == lax.axis_size("col") - 1)
        def _():
            down1_ref[0:DOWN] = last1_ref[...]

        down2_ref[0:PACKED] = last2_ref[...]
        purify(
            total_rows, blocks_ref, cols_ref, up1_ref, up2_ref, down1_ref, down2_ref, *refs
        )


def shifted(value, by):
    devices = lax.axis_size(AXES)
    return lax.ppermute(value, AXES, [(d, (d + by) % devices) for d in range(devices)])


def shifted_down(value, by, near):
    devices, run = lax.axis_size(AXES), lax.axis_size("col")
    inside = range(1, run) if by == 1 else range(2, run - 2)
    pairs = [(d, (d - by) % devices) for d in range(devices) if (d % run in inside) == near]
    return lax.ppermute(value, AXES, pairs)


def on_device(blocks, block_cols, pair_blocks):
    total_rows = ROWS * lax.axis_size(AXES)
    f32 = lambda *shape: jax.ShapeDtypeStruct(shape, F32)
    params = pltpu.CompilerParams(vmem_limit_bytes=48 << 20)
    hbm = pl.BlockSpec(memory_space=pltpu.HBM)
    up, triangle, blocks = pl.pallas_call(
        lambda *refs: pack_up(total_rows, *refs),
        out_shape=(f32(UP, B), f32(PACKED, B), f32(ROWS, NNZ, B, B)),
        in_specs=[hbm, hbm],
        out_specs=(VMEM, VMEM, VMEM),
        scratch_shapes=[
            pltpu.SMEM((ROWS, NNZ), jnp.int32),
            pltpu.SemaphoreType.DMA,
            pltpu.SemaphoreType.DMA,
        ],
        compiler_params=params,
        name="pack_up",
    )(blocks, block_cols)
    up1 = shifted(up, 1)
    up2 = shifted(triangle, 2)
    near1, near2, last1, last2 = pl.pallas_call(
        lambda *refs: pack_down(total_rows, *refs),
        out_shape=(f32(NEAR1, B), f32(NEAR2, B), f32(DOWN, B), f32(PACKED, B)),
        in_specs=[VMEM, SMEM, VMEM],
        out_specs=(VMEM,) * 4,
        compiler_params=params,
        name="pack_down",
    )(blocks, block_cols, triangle)
    down1 = shifted_down(near1, 1, True)
    down2 = shifted_down(near2, 2, True)
    last1 = shifted_down(last1, 1, False)
    last2 = shifted_down(last2, 2, False)
    up1, up2 = pl.pallas_call(
        pass_on,
        out_shape=(f32(UP, B), f32(PACKED, B)),
        in_specs=[ANY] * 2,
        out_specs=(ANY,) * 2,
        input_output_aliases={0: 0, 1: 1},
        compiler_params=params,
        cost_estimate=pl.CostEstimate(flops=4_000_000_000, bytes_accessed=1024, transcendentals=0),
        name="pass_on",
    )(up1, up2)
    window = pltpu.VMEM((SPAN * B, SPAN * B), BF)
    strip = pltpu.VMEM((ROWS * B, SPAN * B), BF)
    work = [window, window, pltpu.VMEM((ROWS * B, SPAN * B), F32), strip, strip]
    work += [pltpu.VMEM((ROWS, NNZ, B, B), F32), pltpu.SemaphoreType.DMA]
    result = pl.pallas_call(
        lambda *refs: purify_most(total_rows, *refs),
        out_shape=f32(ROWS, NNZ, B, B),
        in_specs=[VMEM, SMEM] + [VMEM] * 4,
        out_specs=ANY,
        scratch_shapes=work,
        compiler_params=params,
        name="purify_most",
    )(blocks, block_cols, up1, up2, down1, down2)
    return pl.pallas_call(
        lambda *refs: purify_last(total_rows, *refs),
        out_shape=f32(ROWS, NNZ, B, B),
        in_specs=[VMEM, SMEM] + [VMEM] * 6 + [ANY],
        out_specs=ANY,
        input_output_aliases={8: 0},
        scratch_shapes=work,
        compiler_params=params,
        name="purify_last",
    )(blocks, block_cols, up1, up2, down1, down2, last1, last2, result)


def solution(mesh):
    placed = (
        P(AXES, None, None, None),
        P(AXES, None),
        P(AXES, None, None),
    )
    return jax.shard_map(
        on_device,
        mesh=mesh,
        in_specs=placed,
        out_specs=P(AXES, None, None, None),
        check_vma=False,
    )
```

```python
import jax
import jax.numpy as jnp
from jax import lax
from jax.experimental import pallas as pl
from jax.experimental.pallas import tpu as pltpu
from jax.sharding import PartitionSpec as P

B = 128
NNZ = 8
REACH = 4
ROWS = 2
SPAN = ROWS + 2 * REACH
PAIR = 2 * B
AXES = ("row", "col")
PACKED = 2 * B + 8
DOWN = PACKED + 4 * B
UP = DOWN + 3 * B
LATE = 4
BF, F32 = jnp.bfloat16, jnp.float32
SMEM = pl.BlockSpec(memory_space=pltpu.SMEM)
VMEM = pl.BlockSpec(memory_space=pltpu.VMEM)
ANY = pl.BlockSpec(memory_space=pl.ANY)


def device_index():
    return lax.axis_index("row") * lax.axis_size("col") + lax.axis_index("col")


def missing_of(cols_ref, first_row, total_rows):
    found = []
    for i in range(ROWS):
        count = jnp.int32(0)
        for s in range(NNZ):
            natural = lax.rem(first_row + i + s - REACH + total_rows, total_rows)
            count = count + jnp.where(cols_ref[i, s] == natural, 1, 0)
        found.append(count)
    return found


def known(missing_ref):
    return [missing_ref[i, 0] for i in range(ROWS)]


def held(missing, offset):
    return offset != missing


def slot_of(missing, offset):
    return jnp.minimum(offset - jnp.where(missing < offset, 1, 0), NNZ - 1)


def own_block(blocks_ref, missing, i, offset):
    value = blocks_ref[i, slot_of(missing[i], offset)]
    return jnp.where(held(missing[i], offset), value, 0.0)


def grid_ids():
    return lax.broadcasted_iota(jnp.int32, (B, B), 0), lax.broadcasted_iota(jnp.int32, (B, B), 1)


def write_triangle(blocks_ref, missing, out_ref):
    first = own_block(blocks_ref, missing, 0, REACH)
    second = own_block(blocks_ref, missing, 1, REACH)
    rows, cols = grid_ids()
    out_ref[0:B] = jnp.where(rows <= cols, first, second)
    out_ref[B : 2 * B] = own_block(blocks_ref, missing, 0, REACH + 1)
    diagonal = jnp.sum(jnp.where(rows == cols, second, 0.0), axis=0, keepdims=True)
    out_ref[2 * B : PACKED] = jnp.broadcast_to(diagonal, (PACKED - 2 * B, B))


def read_triangle(ref):
    packed, between = ref[0:B], ref[B : 2 * B]
    turned = packed.T
    rows, cols = grid_ids()
    first = jnp.where(rows <= cols, packed, turned)
    second = jnp.where(rows > cols, packed, jnp.where(rows < cols, turned, ref[2 * B : 2 * B + 1]))
    return first, between, second


def pack_up(
    total_rows, blocks_hbm, cols_hbm, up_ref, tri_ref, blocks_ref, missing_ref, cols_ref, blocks_sem, cols_sem
):
    fetch_cols = pltpu.make_async_copy(cols_hbm, cols_ref, cols_sem)
    fetch_blocks = pltpu.make_async_copy(blocks_hbm, blocks_ref, blocks_sem)
    fetch_cols.start()
    fetch_blocks.start()
    fetch_cols.wait()
    missing = missing_of(cols_ref, device_index() * ROWS, total_rows)
    for i in range(ROWS):
        missing_ref[i : i + 1] = jnp.full((1, B), missing[i], jnp.int32)
    fetch_blocks.wait()
    write_triangle(blocks_ref, missing, tri_ref)
    up_ref[0:PACKED] = tri_ref[...]
    below = ((0, -2), (0, -1), (1, -2), (1, -1))
    across = ((1, 4), (1, 5), (0, 4))
    for n, (i, j) in enumerate(below + across):
        at = PACKED + n * B
        up_ref[at : at + B] = own_block(blocks_ref, missing, i, j - i + REACH)


def pack_down(blocks_ref, missing_ref, tri_in_ref, down1_ref, down2_ref):
    missing = known(missing_ref)
    for ref in (down1_ref, down2_ref):
        ref[0:PACKED] = tri_in_ref[...]
    for n, (i, j) in enumerate(((0, 2), (0, 3), (1, 2), (1, 3))):
        at = PACKED + n * B
        value = own_block(blocks_ref, missing, i, j - i + REACH)
        down1_ref[at : at + B] = value


def pass_four(*refs):
    pass


def pass_on(up1_ref, up2_ref, up1_out_ref, up2_out_ref):
    pass


def tile(n):
    return slice(n * B, (n + 1) * B)


def purify(
    blocks_ref,
    missing_ref,
    up1_ref,
    up2_ref,
    down1_ref,
    down2_ref,
    out_hbm,
    high,
    low,
    square,
    square_high,
    square_low,
    staged,
    out_sem,
):
    missing = known(missing_ref)

    def put(k, j, value):
        top = value.astype(BF)
        high[tile(k), tile(j)] = top
        low[tile(k), tile(j)] = (value - top.astype(F32)).astype(BF)

    def put_both(k, j, value):
        put(k, j, value)
        put(j, k, value.T)

    for i in range(ROWS):
        for offset in range(2 * REACH + 1):
            value = own_block(blocks_ref, missing, i, offset)
            j = i + offset
            if REACH <= j < REACH + ROWS:
                put(REACH + i, j, value)
            else:
                put_both(REACH + i, j, value)
    for ref, at in ((up2_ref, 0), (up1_ref, 2), (down1_ref, 6), (down2_ref, 8)):
        first, between, second = read_triangle(ref)
        put(at, at, first)
        put_both(at, at + 1, between)
        put(at + 1, at + 1, second)
    for n, (k, j) in enumerate(((2, 0), (2, 1), (3, 0), (3, 1))):
        put_both(k, j, up1_ref[PACKED + n * B : PACKED + (n + 1) * B])
    for n, (k, j) in enumerate(((6, 8), (6, 9), (7, 8), (7, 9))):
        put_both(k, j, down1_ref[PACKED + n * B : PACKED + (n + 1) * B])
    for n, (k, j) in enumerate(((3, 6), (3, 7), (2, 6))):
        put_both(k, j, up1_ref[DOWN + n * B : DOWN + (n + 1) * B])
    nothing = jnp.zeros((B, B), BF)
    for k, j in ((0, 5), (2, 7), (4, 9)):
        for part in (high, low):
            part[tile(k), tile(j)] = nothing
            part[tile(j), tile(k)] = nothing

    def product(left_high, left_low, b):
        inner = slice(max(0, b - 2) * PAIR, min(SPAN // 2, b + 3) * PAIR)
        outer = slice(b * PAIR, (b + 1) * PAIR)

        def dot(left, right):
            return jnp.dot(left, right[inner, outer], preferred_element_type=F32)

        return dot(left_high(inner), high) + dot(left_low(inner), high) + dot(left_high(inner), low)

    own = slice(REACH * B, (REACH + ROWS) * B)
    for b in range(SPAN // 2):
        total = product(lambda at: high[own, at], lambda at: low[own, at], b)
        for i in range(ROWS):
            for j in (2 * b, 2 * b + 1):
                value = total[tile(i), tile(j - 2 * b)]
                offset = j - i
                if 0 <= offset <= 2 * REACH:
                    value = jnp.where(held(missing[i], offset), value, 0.0)
                else:
                    value = jnp.zeros_like(value)
                square[tile(i), tile(j)] = value
                top = value.astype(BF)
                square_high[tile(i), tile(j)] = top
                square_low[tile(i), tile(j)] = (value - top.astype(F32)).astype(BF)
    for b in range(SPAN // 2):
        total = product(lambda at: square_high[:, at], lambda at: square_low[:, at], b)
        outer = slice(b * PAIR, (b + 1) * PAIR)
        square[:, outer] = 3.0 * square[:, outer] - 2.0 * total
        for i in range(ROWS):
            for s in range(NNZ):
                if (i + s + 1) // 2 == b:
                    at = pl.multiple_of((i + s + jnp.where(missing[i] <= s, 1, 0)) * B, B)
                    staged[i, s] = square[tile(i), pl.ds(at, B)]
                    pltpu.make_async_copy(staged.at[i, s], out_hbm.at[i, s], out_sem).start()
    pltpu.make_async_copy(staged, out_hbm, out_sem).wait()


def late():
    return lax.axis_index("col") >= lax.axis_size("col") - LATE


def purify_most(*refs):
    @pl.when(jnp.logical_not(late()))
    def _():
        purify(*refs)


def purify_last(
    blocks_ref,
    missing_ref,
    up1_ref,
    up2_ref,
    down1_ref,
    down2_ref,
    last1_ref,
    last2_ref,
    given_ref,
    *refs,
):
    @pl.when(late())
    def _():
        col = lax.axis_index("col") - lax.axis_size("col")

        @pl.when(col == -1)
        def _():
            down1_ref[...] = last1_ref[...]

        down2_ref[...] = last2_ref[...]
        purify(
            blocks_ref, missing_ref, up1_ref, up2_ref, down1_ref, down2_ref, *refs
        )


def shifted(value, by):
    devices = lax.axis_size(AXES)
    return lax.ppermute(value, AXES, [(d, (d + by) % devices) for d in range(devices)])


def shifted_down(value, by, near):
    devices, run = lax.axis_size(AXES), lax.axis_size("col")
    inside = range(1, run) if by == 1 else range(2, run - 2)
    pairs = [(d, (d - by) % devices) for d in range(devices) if (d % run in inside) == near]
    return lax.ppermute(value, AXES, pairs)


def on_device(blocks, block_cols, pair_blocks):
    total_rows = ROWS * lax.axis_size(AXES)
    f32 = lambda *shape: jax.ShapeDtypeStruct(shape, F32)
    params = pltpu.CompilerParams(vmem_limit_bytes=48 << 20)
    hbm = pl.BlockSpec(memory_space=pltpu.HBM)
    up, triangle, blocks, missing = pl.pallas_call(
        lambda *refs: pack_up(total_rows, *refs),
        out_shape=(
            f32(UP, B),
            f32(PACKED, B),
            f32(ROWS, NNZ, B, B),
            jax.ShapeDtypeStruct((8, B), jnp.int32),
        ),
        in_specs=[hbm, hbm],
        out_specs=(VMEM,) * 4,
        scratch_shapes=[
            pltpu.SMEM((ROWS, NNZ), jnp.int32),
            pltpu.SemaphoreType.DMA,
            pltpu.SemaphoreType.DMA,
        ],
        compiler_params=params,
        name="pack_up",
    )(blocks, block_cols)
    up1 = shifted(up, 1)
    up2 = shifted(triangle, 2)
    send1, send2 = pl.pallas_call(
        pack_down,
        out_shape=(f32(DOWN, B), f32(PACKED, B)),
        in_specs=[VMEM] * 3,
        out_specs=(VMEM,) * 2,
        compiler_params=params,
        name="pack_down",
    )(blocks, missing, triangle)
    down1 = shifted_down(send1, 1, True)
    down2 = shifted_down(send2, 2, True)
    down1, down2, send1, send2 = pl.pallas_call(
        pass_four,
        out_shape=tuple(f32(n, B) for n in (DOWN, PACKED, DOWN, PACKED)),
        in_specs=[ANY] * 4,
        out_specs=(ANY,) * 4,
        input_output_aliases={n: n for n in range(4)},
        compiler_params=params,
        name="pass_four",
    )(down1, down2, send1, send2)
    last1 = shifted_down(send1, 1, False)
    last2 = shifted_down(send2, 2, False)
    up1, up2 = pl.pallas_call(
        pass_on,
        out_shape=(f32(UP, B), f32(PACKED, B)),
        in_specs=[ANY] * 2,
        out_specs=(ANY,) * 2,
        input_output_aliases={0: 0, 1: 1},
        compiler_params=params,
        cost_estimate=pl.CostEstimate(flops=4_000_000_000, bytes_accessed=1024, transcendentals=0),
        name="pass_on",
    )(up1, up2)
    window = pltpu.VMEM((SPAN * B, SPAN * B), BF)
    strip = pltpu.VMEM((ROWS * B, SPAN * B), BF)
    work = [window, window, pltpu.VMEM((ROWS * B, SPAN * B), F32), strip, strip]
    work += [pltpu.VMEM((ROWS, NNZ, B, B), F32), pltpu.SemaphoreType.DMA]
    result = pl.pallas_call(
        purify_most,
        out_shape=f32(ROWS, NNZ, B, B),
        in_specs=[VMEM] * 6,
        out_specs=ANY,
        scratch_shapes=work,
        compiler_params=params,
        name="purify_most",
    )(blocks, missing, up1, up2, down1, down2)
    return pl.pallas_call(
        purify_last,
        out_shape=f32(ROWS, NNZ, B, B),
        in_specs=[VMEM] * 8 + [ANY],
        out_specs=ANY,
        input_output_aliases={8: 0},
        scratch_shapes=work,
        compiler_params=params,
        name="purify_last",
    )(blocks, missing, up1, up2, down1, down2, last1, last2, result)


def solution(mesh):
    placed = (
        P(AXES, None, None, None),
        P(AXES, None),
        P(AXES, None, None),
    )
    return jax.shard_map(
        on_device,
        mesh=mesh,
        in_specs=placed,
        out_specs=P(AXES, None, None, None),
        check_vma=False,
    )
```

```python
import jax
import jax.numpy as jnp
from jax import lax
from jax.experimental import pallas as pl
from jax.experimental.pallas import tpu as pltpu
from jax.sharding import PartitionSpec as P

B = 128
NNZ = 8
REACH = 4
ROWS = 2
SPAN = ROWS + 2 * REACH
PAIR = 2 * B
AXES = ("row", "col")
PACKED = 2 * B + 8
DOWN = PACKED + 4 * B
UP = DOWN + 3 * B
LATE = 4
BF, F32 = jnp.bfloat16, jnp.float32
SMEM = pl.BlockSpec(memory_space=pltpu.SMEM)
VMEM = pl.BlockSpec(memory_space=pltpu.VMEM)
ANY = pl.BlockSpec(memory_space=pl.ANY)


def device_index():
    return lax.axis_index("row") * lax.axis_size("col") + lax.axis_index("col")


def missing_of(cols_ref, first_row, total_rows):
    found = []
    for i in range(ROWS):
        count = jnp.int32(0)
        for s in range(NNZ):
            natural = lax.rem(first_row + i + s - REACH + total_rows, total_rows)
            count = count + jnp.where(cols_ref[i, s] == natural, 1, 0)
        found.append(count)
    return found


def known(missing_ref):
    return [missing_ref[i, 0] for i in range(ROWS)]


def held(missing, offset):
    return offset != missing


def slot_of(missing, offset):
    return jnp.minimum(offset - jnp.where(missing < offset, 1, 0), NNZ - 1)


def own_block(blocks_ref, missing, i, offset):
    value = blocks_ref[i, slot_of(missing[i], offset)]
    return jnp.where(held(missing[i], offset), value, 0.0)


def grid_ids():
    return lax.broadcasted_iota(jnp.int32, (B, B), 0), lax.broadcasted_iota(jnp.int32, (B, B), 1)


def write_triangle(blocks_ref, missing, out_ref):
    first = own_block(blocks_ref, missing, 0, REACH)
    second = own_block(blocks_ref, missing, 1, REACH)
    rows, cols = grid_ids()
    out_ref[0:B] = jnp.where(rows <= cols, first, second)
    out_ref[B : 2 * B] = own_block(blocks_ref, missing, 0, REACH + 1)
    diagonal = jnp.sum(jnp.where(rows == cols, second, 0.0), axis=0, keepdims=True)
    out_ref[2 * B : PACKED] = jnp.broadcast_to(diagonal, (PACKED - 2 * B, B))


def read_triangle(ref):
    packed, between = ref[0:B], ref[B : 2 * B]
    turned = packed.T
    rows, cols = grid_ids()
    first = jnp.where(rows <= cols, packed, turned)
    second = jnp.where(rows > cols, packed, jnp.where(rows < cols, turned, ref[2 * B : 2 * B + 1]))
    return first, between, second


def pack_up(total_rows, blocks_ref, cols_ref, up_ref, tri_ref, missing_ref):
    missing = missing_of(cols_ref, device_index() * ROWS, total_rows)
    for i in range(ROWS):
        missing_ref[i : i + 1] = jnp.full((1, B), missing[i], jnp.int32)
    write_triangle(blocks_ref, missing, tri_ref)
    up_ref[0:PACKED] = tri_ref[...]
    below = ((0, -2), (0, -1), (1, -2), (1, -1))
    across = ((1, 4), (1, 5), (0, 4))
    for n, (i, j) in enumerate(below + across):
        at = PACKED + n * B
        up_ref[at : at + B] = own_block(blocks_ref, missing, i, j - i + REACH)


def pack_down(blocks_ref, missing_ref, tri_in_ref, down1_ref, down2_ref):
    missing = known(missing_ref)
    for ref in (down1_ref, down2_ref):
        ref[0:PACKED] = tri_in_ref[...]
    for n, (i, j) in enumerate(((0, 2), (0, 3), (1, 2), (1, 3))):
        at = PACKED + n * B
        value = own_block(blocks_ref, missing, i, j - i + REACH)
        down1_ref[at : at + B] = value


def pass_four(*refs):
    pass


def pass_on(up1_ref, up2_ref, up1_out_ref, up2_out_ref):
    pass


def tile(n):
    return slice(n * B, (n + 1) * B)


def purify(
    blocks_ref,
    missing_ref,
    up1_ref,
    up2_ref,
    down1_ref,
    down2_ref,
    out_hbm,
    high,
    low,
    square,
    square_high,
    square_low,
    staged,
    out_sem,
):
    missing = known(missing_ref)

    def put(k, j, value):
        top = value.astype(BF)
        high[tile(k), tile(j)] = top
        low[tile(k), tile(j)] = (value - top.astype(F32)).astype(BF)

    def put_both(k, j, value):
        put(k, j, value)
        put(j, k, value.T)

    for i in range(ROWS):
        for offset in range(2 * REACH + 1):
            value = own_block(blocks_ref, missing, i, offset)
            j = i + offset
            if REACH <= j < REACH + ROWS:
                put(REACH + i, j, value)
            else:
                put_both(REACH + i, j, value)
    for ref, at in ((up2_ref, 0), (up1_ref, 2), (down1_ref, 6), (down2_ref, 8)):
        first, between, second = read_triangle(ref)
        put(at, at, first)
        put_both(at, at + 1, between)
        put(at + 1, at + 1, second)
    for n, (k, j) in enumerate(((2, 0), (2, 1), (3, 0), (3, 1))):
        put_both(k, j, up1_ref[PACKED + n * B : PACKED + (n + 1) * B])
    for n, (k, j) in enumerate(((6, 8), (6, 9), (7, 8), (7, 9))):
        put_both(k, j, down1_ref[PACKED + n * B : PACKED + (n + 1) * B])
    for n, (k, j) in enumerate(((3, 6), (3, 7), (2, 6))):
        put_both(k, j, up1_ref[DOWN + n * B : DOWN + (n + 1) * B])
    nothing = jnp.zeros((B, B), BF)
    for k, j in ((0, 5), (2, 7), (4, 9)):
        for part in (high, low):
            part[tile(k), tile(j)] = nothing
            part[tile(j), tile(k)] = nothing

    def product(left_high, left_low, b):
        inner = slice(max(0, b - 2) * PAIR, min(SPAN // 2, b + 3) * PAIR)
        outer = slice(b * PAIR, (b + 1) * PAIR)

        def dot(left, right):
            return jnp.dot(left, right[inner, outer], preferred_element_type=F32)

        return dot(left_high(inner), high) + dot(left_low(inner), high) + dot(left_high(inner), low)

    own = slice(REACH * B, (REACH + ROWS) * B)
    for b in range(SPAN // 2):
        total = product(lambda at: high[own, at], lambda at: low[own, at], b)
        for i in range(ROWS):
            for j in (2 * b, 2 * b + 1):
                value = total[tile(i), tile(j - 2 * b)]
                offset = j - i
                if 0 <= offset <= 2 * REACH:
                    value = jnp.where(held(missing[i], offset), value, 0.0)
                else:
                    value = jnp.zeros_like(value)
                square[tile(i), tile(j)] = value
                top = value.astype(BF)
                square_high[tile(i), tile(j)] = top
                square_low[tile(i), tile(j)] = (value - top.astype(F32)).astype(BF)
    for b in range(SPAN // 2):
        total = product(lambda at: square_high[:, at], lambda at: square_low[:, at], b)
        outer = slice(b * PAIR, (b + 1) * PAIR)
        square[:, outer] = 3.0 * square[:, outer] - 2.0 * total
        for i in range(ROWS):
            for s in range(NNZ):
                if (i + s + 1) // 2 == b:
                    at = pl.multiple_of((i + s + jnp.where(missing[i] <= s, 1, 0)) * B, B)
                    staged[i, s] = square[tile(i), pl.ds(at, B)]
                    pltpu.make_async_copy(staged.at[i, s], out_hbm.at[i, s], out_sem).start()
    pltpu.make_async_copy(staged, out_hbm, out_sem).wait()


def late():
    return lax.axis_index("col") >= lax.axis_size("col") - LATE


def purify_most(*refs):
    @pl.when(jnp.logical_not(late()))
    def _():
        purify(*refs)


def purify_last(
    blocks_ref,
    missing_ref,
    up1_ref,
    up2_ref,
    down1_ref,
    down2_ref,
    last1_ref,
    last2_ref,
    given_ref,
    *refs,
):
    @pl.when(late())
    def _():
        col = lax.axis_index("col") - lax.axis_size("col")

        @pl.when(col == -1)
        def _():
            down1_ref[...] = last1_ref[...]

        down2_ref[...] = last2_ref[...]
        purify(
            blocks_ref, missing_ref, up1_ref, up2_ref, down1_ref, down2_ref, *refs
        )


def shifted(value, by):
    devices = lax.axis_size(AXES)
    return lax.ppermute(value, AXES, [(d, (d + by) % devices) for d in range(devices)])


def shifted_down(value, by, near):
    devices, run = lax.axis_size(AXES), lax.axis_size("col")
    inside = range(1, run) if by == 1 else range(2, run - 2)
    pairs = [(d, (d - by) % devices) for d in range(devices) if (d % run in inside) == near]
    return lax.ppermute(value, AXES, pairs)


def on_device(blocks, block_cols, pair_blocks):
    total_rows = ROWS * lax.axis_size(AXES)
    f32 = lambda *shape: jax.ShapeDtypeStruct(shape, F32)
    params = pltpu.CompilerParams(vmem_limit_bytes=48 << 20)
    up, triangle, missing = pl.pallas_call(
        lambda *refs: pack_up(total_rows, *refs),
        out_shape=(f32(UP, B), f32(PACKED, B), jax.ShapeDtypeStruct((8, B), jnp.int32)),
        in_specs=[VMEM, VMEM],
        out_specs=(VMEM,) * 3,
        compiler_params=params,
        name="pack_up",
    )(blocks, block_cols)
    up1 = shifted(up, 1)
    up2 = shifted(triangle, 2)
    send1, send2 = pl.pallas_call(
        pack_down,
        out_shape=(f32(DOWN, B), f32(PACKED, B)),
        in_specs=[VMEM] * 3,
        out_specs=(VMEM,) * 2,
        compiler_params=params,
        name="pack_down",
    )(blocks, missing, triangle)
    down1 = shifted_down(send1, 1, True)
    down2 = shifted_down(send2, 2, True)
    down1, down2, send1, send2 = pl.pallas_call(
        pass_four,
        out_shape=tuple(f32(n, B) for n in (DOWN, PACKED, DOWN, PACKED)),
        in_specs=[ANY] * 4,
        out_specs=(ANY,) * 4,
        input_output_aliases={n: n for n in range(4)},
        compiler_params=params,
        name="pass_four",
    )(down1, down2, send1, send2)
    last1 = shifted_down(send1, 1, False)
    last2 = shifted_down(send2, 2, False)
    up1, up2 = pl.pallas_call(
        pass_on,
        out_shape=(f32(UP, B), f32(PACKED, B)),
        in_specs=[ANY] * 2,
        out_specs=(ANY,) * 2,
        input_output_aliases={0: 0, 1: 1},
        compiler_params=params,
        cost_estimate=pl.CostEstimate(flops=4_000_000_000, bytes_accessed=1024, transcendentals=0),
        name="pass_on",
    )(up1, up2)
    window = pltpu.VMEM((SPAN * B, SPAN * B), BF)
    strip = pltpu.VMEM((ROWS * B, SPAN * B), BF)
    work = [window, window, pltpu.VMEM((ROWS * B, SPAN * B), F32), strip, strip]
    work += [pltpu.VMEM((ROWS, NNZ, B, B), F32), pltpu.SemaphoreType.DMA]
    result = pl.pallas_call(
        purify_most,
        out_shape=f32(ROWS, NNZ, B, B),
        in_specs=[VMEM] * 6,
        out_specs=ANY,
        scratch_shapes=work,
        compiler_params=params,
        name="purify_most",
    )(blocks, missing, up1, up2, down1, down2)
    return pl.pallas_call(
        purify_last,
        out_shape=f32(ROWS, NNZ, B, B),
        in_specs=[VMEM] * 8 + [ANY],
        out_specs=ANY,
        input_output_aliases={8: 0},
        scratch_shapes=work,
        compiler_params=params,
        name="purify_last",
    )(blocks, missing, up1, up2, down1, down2, last1, last2, result)


def solution(mesh):
    placed = (
        P(AXES, None, None, None),
        P(AXES, None),
        P(AXES, None, None),
    )
    return jax.shard_map(
        on_device,
        mesh=mesh,
        in_specs=placed,
        out_specs=P(AXES, None, None, None),
        check_vma=False,
    )
```

```python
import jax
import jax.numpy as jnp
from jax import lax
from jax.experimental import pallas as pl
from jax.experimental.pallas import tpu as pltpu
from jax.sharding import PartitionSpec as P

B = 128
NNZ = 8
REACH = 4
ROWS = 2
SPAN = ROWS + 2 * REACH
PAIR = 2 * B
AXES = ("row", "col")
PACKED = 2 * B + 8
DOWN = PACKED + 4 * B
UP = DOWN + 3 * B
LATE = 4
BF, F32 = jnp.bfloat16, jnp.float32
SMEM = pl.BlockSpec(memory_space=pltpu.SMEM)
VMEM = pl.BlockSpec(memory_space=pltpu.VMEM)
ANY = pl.BlockSpec(memory_space=pl.ANY)


def device_index():
    return lax.axis_index("row") * lax.axis_size("col") + lax.axis_index("col")


def missing_of(cols_ref, first_row, total_rows):
    found = []
    for i in range(ROWS):
        count = jnp.int32(0)
        for s in range(NNZ):
            natural = lax.rem(first_row + i + s - REACH + total_rows, total_rows)
            count = count + jnp.where(cols_ref[i, s] == natural, 1, 0)
        found.append(count)
    return found


def known(missing_ref):
    return [missing_ref[i, 0] for i in range(ROWS)]


def held(missing, offset):
    return offset != missing


def slot_of(missing, offset):
    return jnp.minimum(offset - jnp.where(missing < offset, 1, 0), NNZ - 1)


def own_block(blocks_ref, missing, i, offset):
    value = blocks_ref[i, slot_of(missing[i], offset)]
    return jnp.where(held(missing[i], offset), value, 0.0)


def grid_ids():
    return lax.broadcasted_iota(jnp.int32, (B, B), 0), lax.broadcasted_iota(jnp.int32, (B, B), 1)


def write_triangle(blocks_ref, missing, out_ref):
    first = own_block(blocks_ref, missing, 0, REACH)
    second = own_block(blocks_ref, missing, 1, REACH)
    rows, cols = grid_ids()
    out_ref[0:B] = jnp.where(rows <= cols, first, second)
    out_ref[B : 2 * B] = own_block(blocks_ref, missing, 0, REACH + 1)
    diagonal = jnp.sum(jnp.where(rows == cols, second, 0.0), axis=0, keepdims=True)
    out_ref[2 * B : PACKED] = jnp.broadcast_to(diagonal, (PACKED - 2 * B, B))


def read_triangle(ref):
    packed, between = ref[0:B], ref[B : 2 * B]
    turned = packed.T
    rows, cols = grid_ids()
    first = jnp.where(rows <= cols, packed, turned)
    second = jnp.where(rows > cols, packed, jnp.where(rows < cols, turned, ref[2 * B : 2 * B + 1]))
    return first, between, second


def pack_up(total_rows, blocks_ref, cols_ref, up_ref, tri_ref, missing_ref):
    missing = missing_of(cols_ref, device_index() * ROWS, total_rows)
    for i in range(ROWS):
        missing_ref[i : i + 1] = jnp.full((1, B), missing[i], jnp.int32)
    write_triangle(blocks_ref, missing, tri_ref)
    up_ref[0:PACKED] = tri_ref[...]
    below = ((0, -2), (0, -1), (1, -2), (1, -1))
    across = ((1, 4), (1, 5), (0, 4))
    for n, (i, j) in enumerate(below + across):
        at = PACKED + n * B
        up_ref[at : at + B] = own_block(blocks_ref, missing, i, j - i + REACH)


def pack_down(blocks_ref, missing_ref, tri_in_ref, down1_ref, down2_ref):
    missing = known(missing_ref)
    for ref in (down1_ref, down2_ref):
        ref[0:PACKED] = tri_in_ref[...]
    for n, (i, j) in enumerate(((0, 2), (0, 3), (1, 2), (1, 3))):
        at = PACKED + n * B
        value = own_block(blocks_ref, missing, i, j - i + REACH)
        down1_ref[at : at + B] = value


def pass_four(*refs):
    pass


def pass_on(up1_ref, up2_ref, up1_out_ref, up2_out_ref):
    pass


def tile(n):
    return slice(n * B, (n + 1) * B)


def purify(
    blocks_ref,
    missing_ref,
    up1_ref,
    up2_ref,
    down1_ref,
    down2_ref,
    out_hbm,
    high,
    low,
    square,
    square_high,
    square_low,
    staged,
    out_sem,
):
    missing = known(missing_ref)

    def put(k, j, value):
        top = value.astype(BF)
        high[tile(k), tile(j)] = top
        low[tile(k), tile(j)] = (value - top.astype(F32)).astype(BF)

    def put_both(k, j, value):
        put(k, j, value)
        put(j, k, value.T)

    def product(left_high, left_low, b):
        inner = slice(max(0, b - 2) * PAIR, min(SPAN // 2, b + 3) * PAIR)
        outer = slice(b * PAIR, (b + 1) * PAIR)

        def dot(left, right):
            return jnp.dot(left, right[inner, outer], preferred_element_type=F32)

        return dot(left_high(inner), high) + dot(left_low(inner), high) + dot(left_high(inner), low)

    own = slice(REACH * B, (REACH + ROWS) * B)
    def first_product(b):
        total = product(lambda at: high[own, at], lambda at: low[own, at], b)
        for i in range(ROWS):
            for j in (2 * b, 2 * b + 1):
                value = total[tile(i), tile(j - 2 * b)]
                offset = j - i
                if 0 <= offset <= 2 * REACH:
                    value = jnp.where(held(missing[i], offset), value, 0.0)
                else:
                    value = jnp.zeros_like(value)
                square[tile(i), tile(j)] = value
                top = value.astype(BF)
                square_high[tile(i), tile(j)] = top
                square_low[tile(i), tile(j)] = (value - top.astype(F32)).astype(BF)

    nothing = jnp.zeros((B, B), BF)
    for k, j in ((0, 5), (2, 7), (4, 9)):
        for part in (high, low):
            part[tile(k), tile(j)] = nothing
            part[tile(j), tile(k)] = nothing

    for i in range(ROWS):
        for offset in range(2 * REACH + 1):
            value = own_block(blocks_ref, missing, i, offset)
            j = i + offset
            if REACH <= j < REACH + ROWS:
                put(REACH + i, j, value)
            else:
                put_both(REACH + i, j, value)
    first_product(2)
    for ref, at in ((up2_ref, 0), (up1_ref, 2), (down1_ref, 6), (down2_ref, 8)):
        first, between, second = read_triangle(ref)
        put(at, at, first)
        put_both(at, at + 1, between)
        put(at + 1, at + 1, second)
    for n, (k, j) in enumerate(((2, 0), (2, 1), (3, 0), (3, 1))):
        put_both(k, j, up1_ref[PACKED + n * B : PACKED + (n + 1) * B])
    for n, (k, j) in enumerate(((6, 8), (6, 9), (7, 8), (7, 9))):
        put_both(k, j, down1_ref[PACKED + n * B : PACKED + (n + 1) * B])
    for n, (k, j) in enumerate(((3, 6), (3, 7), (2, 6))):
        put_both(k, j, up1_ref[DOWN + n * B : DOWN + (n + 1) * B])
    for b in (1, 3, 0, 4):
        first_product(b)
    for b in range(SPAN // 2):
        total = product(lambda at: square_high[:, at], lambda at: square_low[:, at], b)
        outer = slice(b * PAIR, (b + 1) * PAIR)
        square[:, outer] = 3.0 * square[:, outer] - 2.0 * total
        for i in range(ROWS):
            for s in range(NNZ):
                if (i + s + 1) // 2 == b:
                    at = pl.multiple_of((i + s + jnp.where(missing[i] <= s, 1, 0)) * B, B)
                    staged[i, s] = square[tile(i), pl.ds(at, B)]
                    pltpu.make_async_copy(staged.at[i, s], out_hbm.at[i, s], out_sem).start()
    pltpu.make_async_copy(staged, out_hbm, out_sem).wait()


def late():
    return lax.axis_index("col") >= lax.axis_size("col") - LATE


def purify_most(*refs):
    @pl.when(jnp.logical_not(late()))
    def _():
        purify(*refs)


def purify_last(
    blocks_ref,
    missing_ref,
    up1_ref,
    up2_ref,
    down1_ref,
    down2_ref,
    last1_ref,
    last2_ref,
    given_ref,
    *refs,
):
    @pl.when(late())
    def _():
        col = lax.axis_index("col") - lax.axis_size("col")

        @pl.when(col == -1)
        def _():
            down1_ref[...] = last1_ref[...]

        down2_ref[...] = last2_ref[...]
        purify(
            blocks_ref, missing_ref, up1_ref, up2_ref, down1_ref, down2_ref, *refs
        )


def shifted(value, by):
    devices = lax.axis_size(AXES)
    return lax.ppermute(value, AXES, [(d, (d + by) % devices) for d in range(devices)])


def shifted_down(value, by, near):
    devices, run = lax.axis_size(AXES), lax.axis_size("col")
    inside = range(1, run) if by == 1 else range(2, run - 2)
    pairs = [(d, (d - by) % devices) for d in range(devices) if (d % run in inside) == near]
    return lax.ppermute(value, AXES, pairs)


def on_device(blocks, block_cols, pair_blocks):
    total_rows = ROWS * lax.axis_size(AXES)
    f32 = lambda *shape: jax.ShapeDtypeStruct(shape, F32)
    params = pltpu.CompilerParams(vmem_limit_bytes=48 << 20)
    up, triangle, missing = pl.pallas_call(
        lambda *refs: pack_up(total_rows, *refs),
        out_shape=(f32(UP, B), f32(PACKED, B), jax.ShapeDtypeStruct((8, B), jnp.int32)),
        in_specs=[VMEM, VMEM],
        out_specs=(VMEM,) * 3,
        compiler_params=params,
        name="pack_up",
    )(blocks, block_cols)
    up1 = shifted(up, 1)
    up2 = shifted(triangle, 2)
    send1, send2 = pl.pallas_call(
        pack_down,
        out_shape=(f32(DOWN, B), f32(PACKED, B)),
        in_specs=[VMEM] * 3,
        out_specs=(VMEM,) * 2,
        compiler_params=params,
        name="pack_down",
    )(blocks, missing, triangle)
    down1 = shifted_down(send1, 1, True)
    down2 = shifted_down(send2, 2, True)
    down1, down2, send1, send2 = pl.pallas_call(
        pass_four,
        out_shape=tuple(f32(n, B) for n in (DOWN, PACKED, DOWN, PACKED)),
        in_specs=[ANY] * 4,
        out_specs=(ANY,) * 4,
        input_output_aliases={n: n for n in range(4)},
        compiler_params=params,
        name="pass_four",
    )(down1, down2, send1, send2)
    last1 = shifted_down(send1, 1, False)
    last2 = shifted_down(send2, 2, False)
    up1, up2 = pl.pallas_call(
        pass_on,
        out_shape=(f32(UP, B), f32(PACKED, B)),
        in_specs=[ANY] * 2,
        out_specs=(ANY,) * 2,
        input_output_aliases={0: 0, 1: 1},
        compiler_params=params,
        cost_estimate=pl.CostEstimate(flops=4_000_000_000, bytes_accessed=1024, transcendentals=0),
        name="pass_on",
    )(up1, up2)
    window = pltpu.VMEM((SPAN * B, SPAN * B), BF)
    strip = pltpu.VMEM((ROWS * B, SPAN * B), BF)
    work = [window, window, pltpu.VMEM((ROWS * B, SPAN * B), F32), strip, strip]
    work += [pltpu.VMEM((ROWS, NNZ, B, B), F32), pltpu.SemaphoreType.DMA]
    result = pl.pallas_call(
        purify_most,
        out_shape=f32(ROWS, NNZ, B, B),
        in_specs=[VMEM] * 6,
        out_specs=ANY,
        scratch_shapes=work,
        compiler_params=params,
        name="purify_most",
    )(blocks, missing, up1, up2, down1, down2)
    return pl.pallas_call(
        purify_last,
        out_shape=f32(ROWS, NNZ, B, B),
        in_specs=[VMEM] * 8 + [ANY],
        out_specs=ANY,
        input_output_aliases={8: 0},
        scratch_shapes=work,
        compiler_params=params,
        name="purify_last",
    )(blocks, missing, up1, up2, down1, down2, last1, last2, result)


def solution(mesh):
    placed = (
        P(AXES, None, None, None),
        P(AXES, None),
        P(AXES, None, None),
    )
    return jax.shard_map(
        on_device,
        mesh=mesh,
        in_specs=placed,
        out_specs=P(AXES, None, None, None),
        check_vma=False,
    )
```
